32 devices in a mesh: section: 2 (over core), batch: 4 (over z), mp: 4 (over y, x).
Axes of the slice: x: 2, y: 2, z: 4, core: 2. Of those that a mesh axis runs over, the one named last changes fastest.
Arguments:
- encoder_in: bfloat16 [4, 6, 256, 768], P('batch', None, 'mp'), may hold values from -6 to 6
- context_lengths: int32 [4, 6, 4], P('batch'), may hold values from 1 to 128, 256 in all within a row
- target_lengths: int32 [4, 6, 4], P('batch'), may hold values from 1 to 64, 128 in all within a row
- target_places: int32 [4, 6, 128], P('batch', None, 'mp'), may hold values from 0 to 783
- encoder_norm1: float32 [768], replicated, may hold values from 0.25 to 1.75
- encoder_qkv: bfloat16 [3, 768, 768], P(None, None, 'mp'), may hold values from -0.21875 to 0.21875
- encoder_proj: bfloat16 [768, 768], P('mp'), may hold values from -1.25 to 1.25
- encoder_norm2: float32 [768], replicated, may hold values from 0.25 to 1.75
- encoder_up: bfloat16 [768, 3072], P(None, 'mp'), may hold values from -0.21875 to 0.21875
- encoder_down: bfloat16 [3072, 768], P('mp'), may hold values from -0.109375 to 0.109375
- link_weight: bfloat16 [768, 384], replicated, may hold values from -0.21875 to 0.21875
- mask_token: float32 [384], replicated, may hold values from -4 to 4
- predictor_norm1: float32 [384], replicated, may hold values from 0.25 to 1.75
- predictor_qkv: bfloat16 [3, 384, 384], P(None, None, 'mp'), may hold values from -0.3125 to 0.3125
- predictor_proj: bfloat16 [384, 384], P('mp'), may hold values from -1.75 to 1.75
- predictor_norm2: float32 [384], replicated, may hold values from 0.25 to 1.75
- predictor_up: bfloat16 [384, 1536], P(None, 'mp'), may hold values from -0.3125 to 0.3125
- predictor_down: bfloat16 [1536, 384], P('mp'), may hold values from -0.15625 to 0.15625
- cotangent: bfloat16 [4, 6, 128, 384], P('batch', None, 'mp'), may hold values from -6 to 6
Outputs:
- encoder_in_grad: float32 [4, 6, 256, 768], P('batch', 'section', 'mp')
- encoder_norm1_grad: float32 [768], replicated
- encoder_qkv_grad: float32 [3, 768, 768], P(None, ('section', 'batch'), 'mp')
- encoder_proj_grad: float32 [768, 768], P('mp', ('section', 'batch'))
- encoder_norm2_grad: float32 [768], replicated
- encoder_up_grad: float32 [768, 3072], P(('section', 'batch'), 'mp')
- encoder_down_grad: float32 [3072, 768], P('mp', ('section', 'batch'))
- link_grad: float32 [768, 384], replicated
- mask_grad: float32 [384], replicated
- predictor_norm1_grad: float32 [384], replicated
- predictor_qkv_grad: float32 [3, 384, 384], P(None, ('section', 'batch'), 'mp')
- predictor_proj_grad: float32 [384, 384], P('mp', ('section', 'batch'))
- predictor_norm2_grad: float32 [384], replicated
- predictor_up_grad: float32 [384, 1536], P(('section', 'batch'), 'mp')
- predictor_down_grad: float32 [1536, 384], P('mp', ('section', 'batch'))
The draws below stay inside these ranges and needn't reach their ends.
Inputs may be any that keep to these rules, and one draw needn't show every extreme that they name: `context_lengths`: in every micro-batch the 4 lengths sum to 256 and the longest is exactly 128. `target_lengths`: in every micro-batch the 4 lengths sum to 128 and the longest is exactly 64.
All inputs are finite; a program needn't handle non-finite values.
Results may differ from the reference program's by a relative error of at most 0.04.
Values may be sent and summed in bfloat16 or wider, within the bound.
A program may use at most 256 MiB of HBM per device.

```python
import math
import jax
import jax.numpy as jnp
import numpy as np
from jax import lax

D = 768
HEADS = 12
FF = 3072
PD = 384
PHEADS = 12
PFF = 1536
PATCHES = 784
IMGS = 4
MB = 6
CAP_C = 256
CAP_T = 128
GROUPS = 4


def place_ends(entries, own_key, low, high):
    longest = entries.shape.index(max(entries.shape))
    spots = []
    for shift in (0, 1):
        where = [jax.random.randint(jax.random.fold_in(own_key, axis), (), 0, length) for axis, length in enumerate(entries.shape)]
        where[longest] = (where[longest] + shift) % entries.shape[longest]
        spots.append(tuple(where))
    return entries.at[spots[0]].set(low).at[spots[1]].set(high)


def level_of(key, shape, split, least, top_value):
    loudness = 1.0
    for dim, parts in split:
        draws = jax.random.uniform(jax.random.fold_in(jax.random.fold_in(key, 6), dim), (parts,), jnp.float32, least / len(split), top_value / len(split))
        loudness = loudness * jnp.repeat(jnp.exp(draws), shape[dim] // parts).reshape((-1,) + (1,) * (len(shape) - 1 - dim))
    return loudness


def split_up(count, total, reach, skew):
    weights = [(1 << 20) // math.isqrt(standing ** skew) + 1 for standing in range(2, count + 1)]
    spare, counts = total - reach - (count - 1), [1] * (count - 1)
    while spare > 0:
        movable = [i for i in range(count - 1) if counts[i] < reach]
        mass, left = sum([weights[i] for i in movable]), spare
        for i in movable:
            addition = min(reach - counts[i], max(1, left * weights[i] // mass), spare)
            counts[i] = counts[i] + addition
            spare = spare - addition
    return np.array([reach] + counts)


def ragged(key, number_of, total, reach, slope):
    if number_of == 2:
        one = jax.random.randint(key, (), max(1, total - reach), min(reach, total - 1) + 1)
        return jnp.stack([one, total - one])
    tallies = jnp.asarray(split_up(number_of, total, reach, slope), jnp.int32)
    pairs = (number_of - 1) // 2
    source_of, receiver = tallies[1:1 + 2 * pairs:2], tallies[2:2 + 2 * pairs:2]
    room = jnp.minimum(source_of - 1, reach - receiver)
    passed = jax.random.randint(jax.random.fold_in(key, 1), (pairs,), 0, 1 << 20) % (room + 1)
    tallies = tallies.at[1:1 + 2 * pairs:2].set(source_of - passed).at[2:2 + 2 * pairs:2].set(receiver + passed)
    return tallies[jax.random.permutation(jax.random.fold_in(key, 2), number_of)]


def normal_values(own_key, shape, scale, most, cuts=(), kind=jnp.bfloat16):
    entries = jax.random.normal(own_key, shape, jnp.float32) * scale
    if len(cuts) > 0:
        entries = level_of(own_key, shape, cuts, -0.22, 0.18) * entries
    return jnp.clip(entries, min=-most, max=most).astype(kind)


def setup_inputs(seed: int = 0) -> dict:
    keys = jax.random.split(jax.random.key(seed), 20)
    encoder_in = normal_values(keys[0], (GROUPS, MB, CAP_C, D), 1.0, 6.0, ((0, 4), (2, 4)))
    context_lengths = jax.vmap(lambda own: ragged(own, IMGS, CAP_C, CAP_C // 2, 2))(jax.random.split(keys[1], GROUPS * MB)).reshape((GROUPS, MB, IMGS)).astype(jnp.int32)
    target_lengths = jax.vmap(lambda own: ragged(own, IMGS, CAP_T, CAP_T // 2, 2))(jax.random.split(keys[2], GROUPS * MB)).reshape((GROUPS, MB, IMGS)).astype(jnp.int32)
    target_places = place_ends(jax.random.randint(keys[3], (GROUPS, MB, CAP_T), 0, PATCHES), jax.random.fold_in(keys[3], 1), 0, PATCHES - 1).astype(jnp.int32)
    encoder_norm1 = jnp.clip(1.0 + 0.15 * jax.random.normal(keys[4], (D,), jnp.float32), 0.25, 1.75)
    encoder_qkv = normal_values(keys[5], (3, D, D), D ** -0.5, 0.21875, ((2, 4),))
    encoder_proj = normal_values(keys[6], (D, D), (D // 32) ** -0.5, 1.25, ((0, 4),))
    encoder_norm2 = jnp.clip(1.0 + 0.15 * jax.random.normal(keys[7], (D,), jnp.float32), 0.25, 1.75)
    encoder_up = normal_values(keys[8], (D, FF), D ** -0.5, 0.21875, ((1, 4),))
    encoder_down = normal_values(keys[9], (FF, D), FF ** -0.5, 0.109375, ((0, 4),))
    link_weight = normal_values(keys[10], (D, PD), D ** -0.5, 0.21875)
    mask_token = normal_values(keys[11], (PD,), 1.0, 4.0, (), jnp.float32)
    predictor_norm1 = jnp.clip(1.0 + 0.15 * jax.random.normal(keys[12], (PD,), jnp.float32), 0.25, 1.75)
    predictor_qkv = normal_values(keys[13], (3, PD, PD), PD ** -0.5, 0.3125, ((2, 4),))
    predictor_proj = normal_values(keys[14], (PD, PD), (PD // 32) ** -0.5, 1.75, ((0, 4),))
    predictor_norm2 = jnp.clip(1.0 + 0.15 * jax.random.normal(keys[15], (PD,), jnp.float32), 0.25, 1.75)
    predictor_up = normal_values(keys[16], (PD, PFF), PD ** -0.5, 0.3125, ((1, 4),))
    predictor_down = normal_values(keys[17], (PFF, PD), PFF ** -0.5, 0.15625, ((0, 4),))
    cotangent = normal_values(keys[18], (GROUPS, MB, CAP_T, PD), 1.0, 6.0, ((0, 4), (2, 4)))
    return dict(encoder_in=encoder_in, context_lengths=context_lengths, target_lengths=target_lengths, target_places=target_places, encoder_norm1=encoder_norm1, encoder_qkv=encoder_qkv, encoder_proj=encoder_proj, encoder_norm2=encoder_norm2, encoder_up=encoder_up, encoder_down=encoder_down, link_weight=link_weight, mask_token=mask_token, predictor_norm1=predictor_norm1, predictor_qkv=predictor_qkv, predictor_proj=predictor_proj, predictor_norm2=predictor_norm2, predictor_up=predictor_up, predictor_down=predictor_down, cotangent=cotangent)


NORM_EPSILON = 1e-06
HIGHEST = lax.Precision.HIGHEST

@jax.custom_vjp
def low(v):
    return lax.optimization_barrier(v.astype(jnp.bfloat16)).astype(jnp.float32)

@jax.custom_vjp
def low_back(v):
    return v

def low_keep(v):
    return (low(v), None)

def low_pass(kept, grad):
    return (grad,)

def back_keep(v):
    return (v, None)

def back_low(kept, grad):
    return (low(grad),)
low.defvjp(low_keep, low_pass)
low_back.defvjp(back_keep, back_low)

def matmul(left, right):
    return jnp.dot(left, right, precision=HIGHEST)

def layer_norm(values, gain_vec):
    average = lax.optimization_barrier(jnp.mean(values, axis=-1, keepdims=True))
    centred = values - average
    variance = lax.optimization_barrier(jnp.mean(centred * centred, axis=-1, keepdims=True))
    return centred * lax.rsqrt(variance + NORM_EPSILON) * gain_vec

def segment_of(lengths, length_all):
    boundary = jnp.cumsum(lengths).astype(jnp.int32)
    places = jnp.arange(length_all, dtype=jnp.int32)
    return lax.optimization_barrier(jnp.sum((places[:, None] >= boundary[None, :]).astype(jnp.int32), axis=1))

def position_code(places, features):
    half_width = features // 2
    frequency = jnp.exp(jnp.arange(half_width, dtype=jnp.float32) * (-2.0 * math.log(10000.0) / features))
    angles = places.astype(jnp.float32)[:, None] * frequency[None, :]
    return jnp.concatenate([jnp.sin(angles), jnp.cos(angles)], axis=1)

def attend(normed, qkv_weight, proj_weight, segments, head_count):
    length_all, features = normed.shape
    head_size = features // head_count
    queries = low_back(low(matmul(normed, qkv_weight[0]))).reshape(length_all, head_count, head_size)
    key_rows = low_back(low(matmul(normed, qkv_weight[1]))).reshape(length_all, head_count, head_size)
    value_rows = low_back(low(matmul(normed, qkv_weight[2]))).reshape(length_all, head_count, head_size)
    scores = jnp.einsum('qhd,khd->hqk', queries, key_rows, precision=HIGHEST) * head_size ** (-0.5)
    scores = low_back(scores)
    allowed = segments[:, None] == segments[None, :]
    scores = jnp.where(allowed[None], scores, -1e+30)
    row_peak = lax.optimization_barrier(jnp.max(scores, axis=-1, keepdims=True))
    raised = jnp.exp(scores - row_peak)
    attn_weights = low(raised / lax.optimization_barrier(jnp.sum(raised, axis=-1, keepdims=True)))
    mixture = jnp.einsum('hqk,khd->qhd', attn_weights, value_rows, precision=HIGHEST).reshape(length_all, features)
    mixture = low_back(low(mixture))
    return low_back(matmul(mixture, proj_weight))

def residual_block(token_rows, weights, segments, head_count):
    norm_one, qkv_weight, proj_weight, norm_two, up_weight, down_weight = weights
    normed = low(layer_norm(token_rows, norm_one))
    midway = token_rows + attend(normed, qkv_weight, proj_weight, segments, head_count)
    normed_two = low(layer_norm(midway, norm_two))
    lifted = low_back(matmul(normed_two, up_weight))
    hidden = low(jax.nn.gelu(lifted, approximate=False))
    return midway + low_back(matmul(hidden, down_weight))

def reference(encoder_in, context_lengths, target_lengths, target_places, encoder_norm1, encoder_qkv, encoder_proj, encoder_norm2, encoder_up, encoder_down, link_weight, mask_token, predictor_norm1, predictor_qkv, predictor_proj, predictor_norm2, predictor_up, predictor_down, cotangent):
    parameters = tuple((weight_arr.astype(jnp.float32) for weight_arr in (encoder_norm1, encoder_qkv, encoder_proj, encoder_norm2, encoder_up, encoder_down, link_weight, mask_token, predictor_norm1, predictor_qkv, predictor_proj, predictor_norm2, predictor_up, predictor_down)))
    buffers = GROUPS * MB
    inputs = encoder_in.astype(jnp.float32).reshape(buffers, CAP_C, D)
    context_all = context_lengths.reshape(buffers, IMGS)
    target_all = target_lengths.reshape(buffers, IMGS)
    places_all = target_places.reshape(buffers, CAP_T)

    def forward(inputs_in, weights_in):
        encoder_weights = weights_in[0:6]
        link_in = weights_in[6]
        mask_in = weights_in[7]
        predictor_weights = weights_in[8:14]

        def one_buffer(element):
            token_rows, context_one, target_one, places_one = element
            context_segments = segment_of(context_one, CAP_C)
            target_segments = segment_of(target_one, CAP_T)
            encoded = low_back(low(residual_block(token_rows, encoder_weights, context_segments, HEADS)))
            context = low_back(matmul(encoded, link_in))
            masked = mask_in[None, :] + position_code(places_one, PD)
            joined = jnp.concatenate([context, masked], axis=0)
            segments = jnp.concatenate([context_segments, target_segments], axis=0)
            predicted = residual_block(joined, predictor_weights, segments, PHEADS)
            return predicted[CAP_C:]
        return lax.map(jax.checkpoint(one_buffer), (inputs_in, context_all, target_all, places_all))
    outputs, pullback = jax.vjp(forward, inputs, parameters)
    input_grad, weight_grads = pullback(cotangent.astype(jnp.float32).reshape(buffers, CAP_T, PD))
    return (input_grad.reshape(GROUPS, MB, CAP_C, D), weight_grads[0], weight_grads[1], weight_grads[2], weight_grads[3], weight_grads[4], weight_grads[5], weight_grads[6], weight_grads[7], weight_grads[8], weight_grads[9], weight_grads[10], weight_grads[11], weight_grads[12], weight_grads[13])
```

```python
import functools
import math

import jax
import jax.numpy as jnp
from jax import lax
from jax.experimental import pallas as pl
from jax.experimental.pallas import tpu as pltpu
from jax.sharding import PartitionSpec as P

HEADS = 12
PHEADS = 12
CAP_C = 256
CAP_T = 128
IMGS = 4
EPS = 1e-6
LOG2E = math.log2(math.e)
MESH = pl.DeviceIdType.MESH
F32 = jnp.float32
BF16 = jnp.bfloat16

(
    AG_H1, RS_O, AG_H2, RS_A, AG_P1, RS_PO, AG_P2, AG_COT, RS_P2, AG_PB, RS_P1,
    AG_DY, RS_2, AG_B, RS_1, AG_PIN,
) = range(16)
N_PHASE = 16
DIRECT = (8, 9)
Z_FIRST = (2, 8)
N_ACT = 56


def mm(a, b):
    return lax.dot_general(a, b, (((1,), (0,)), ((), ())), preferred_element_type=F32)


def mm_nt(a, b):
    return lax.dot_general(a, b, (((1,), (1,)), ((), ())), preferred_element_type=F32)


def mm_tn(a, b):
    return lax.dot_general(a, b, (((0,), (0,)), ((), ())), preferred_element_type=F32)


def mean_of(x):
    return jnp.sum(x, axis=-1, keepdims=True) * (1.0 / x.shape[-1])


def norm_parts(x):
    cen = x - mean_of(x)
    rstd = lax.rsqrt(mean_of(cen * cen) + EPS)
    return cen * rstd, rstd


def norm_forward(x, gain):
    return norm_parts(x)[0] * gain


def norm_backward(x, gain, dh):
    xhat, rstd = norm_parts(x)
    dxh = dh * gain
    dx = rstd * (dxh - mean_of(dxh) - xhat * mean_of(dxh * xhat))
    return dx, dh * xhat


def fold(values):
    total = values[0:8]
    for top in range(8, values.shape[0], 8):
        total = total + values[top:top + 8]
    return total


def reciprocal(x):
    guess = pl.reciprocal(x, approx=True)
    return guess * (2.0 - x * guess)


def turns(angle):
    quarter = jnp.floor(angle * (2.0 / math.pi) + 0.5)
    rest = (angle - quarter * 1.5703125) - quarter * (math.pi / 2 - 1.5703125)
    sq = rest * rest
    sine = rest + rest * sq * (
        -1.0 / 6 + sq * (1.0 / 120 + sq * (-1.0 / 5040 + sq * (1.0 / 362880)))
    )
    cosine = 1.0 + sq * (
        -0.5 + sq * (1.0 / 24 + sq * (-1.0 / 720 + sq * (1.0 / 40320 - sq * (1.0 / 3628800))))
    )
    turn = quarter - 4.0 * jnp.floor(quarter * 0.25)
    odd = jnp.logical_or(turn == 1.0, turn == 3.0)
    first = jnp.where(odd, cosine, sine)
    second = jnp.where(odd, sine, cosine)
    return (
        jnp.where(turn >= 2.0, -first, first),
        jnp.where(jnp.logical_or(turn == 1.0, turn == 2.0), -second, second),
    )


ERF = (0.254829592, -0.284496736, 1.421413741, -1.453152027, 1.061405429)
ERF_P = 0.3275911


def gelu_parts(u):
    bell = jnp.exp(u * u * -0.5)
    below = 1.0 + jnp.abs(u) * (ERF_P * math.sqrt(0.5))
    w = reciprocal(below)
    poly = 0.5 * ERF[4]
    for coefficient in ERF[3::-1]:
        poly = poly * w + 0.5 * coefficient
    tail = poly * w * bell
    phi = jnp.where(u >= 0.0, 1.0 - tail, tail)
    return u * phi, phi + u * bell * (1.0 / math.sqrt(2.0 * math.pi))


def head_mask(width, size, head):
    lane = lax.broadcasted_iota(jnp.int32, (1, width), 1)
    inside = jnp.logical_and(lane >= head * size, lane < (head + 1) * size)
    return jnp.where(inside, 1.0, 0.0).astype(BF16)


def segment(place, bounds):
    place = place.astype(F32)
    total = jnp.zeros(place.shape, F32)
    for bound in bounds:
        total = total + jnp.where(place >= bound, 1.0, 0.0)
    return total


def bounds_of(ref, row):
    lengths = ref[0].astype(F32)
    lane = lax.broadcasted_iota(jnp.int32, lengths.shape, 1)
    own = jnp.sum(jnp.where(lane == row, lengths, 0.0), axis=1, keepdims=True)
    ends = []
    total = jnp.zeros((1, 1), F32)
    for i in range(IMGS):
        total = total + own[i:i + 1, :]
        ends.append(total)
    return ends


def mega(
    nb, z_inside,
    ctx_len, tgt_len, places, x_ref, cot_ref, gain_e1, gain_e2, mask_token, gain_p1, gain_p2,
    *rest,
):
    n_weight = 9
    n_out = 8
    n_grad = 9
    n_minor = 5
    w_hbm = rest[:n_weight]
    rest = rest[n_weight:]
    dx_out = rest[0]
    grad_out = rest[1:1 + n_out]
    l_all = rest[1 + n_out]
    minor_out = rest[2 + n_out:2 + n_out + n_minor]
    rest = rest[2 + n_out + n_minor:]
    w_vmem = rest[:n_weight]
    eqkv, eproj, eup, edown, link, pqkv, pproj, pup, pdown = w_vmem
    w_sem, wys, wyr, wzs, wzr, wcs, wcr = rest[n_weight:n_weight + 7]
    rest = rest[n_weight + 7:]
    (
        xin, cin, pin, h1g, q_s, kv_s, o_s, p_a, p_b, part, rb_o, x1_s, h2g, a_s, gp_s, rb_a,
        y_s, z_s, ph1g, pt1, pq_s, pkv_s, po_s, pp_a, pp_b, part_p, rb_po, m_s, px1_s, ph2g,
        pa_s, cotg, pdu_s, rb_p2, pdbg, pdq_s, pdkv_s, pdkv_acc, pdkv_x, pdkv_r,
        part_p1, rb_p1, dcg, dyg, rb_2, dx1_s, dbg, dqkv_s, dkv_acc, dkv_x, dkv_r,
        rb_1, dx_s, dx_r, ds_s, pds_s,
    ) = rest[:N_ACT]
    rest = rest[N_ACT:]
    g_full = rest[0:n_grad]
    g_core = rest[n_grad:2 * n_grad]
    g_y = rest[2 * n_grad:3 * n_grad]
    g_z = rest[3 * n_grad:4 * n_grad]
    (
        l_full, l_core, l_half, l_mp, l_z,
        minor, m_core, m_mp, m_z,
        ss, rs, ins, inr, inl, kvs, kvr, dxs, dxr,
        gcs, gcr, gys, gyr, gzs, gzr, lcs, lcr, lms, lmr, lzs, lzr, las, lar,
        mcs, mcr, mms, mmr, mzs, mzr,
    ) = rest[4 * n_grad:]

    n_mp = 4
    r = lax.axis_index("mp")
    s = lax.axis_index("section")
    z = lax.axis_index("batch")
    x = lax.rem(r, 2)
    y = lax.div(r, 2)
    x_peer = r + 1 - 2 * x
    y_peer = r + 2 - 4 * y
    other = 1 - s
    pair = lax.rem(z, 2)
    z_pair = z + 1 - 2 * pair
    nm = h1g.shape[0]
    base = y * nm
    W = x_ref.shape[-1]
    PW = cot_ref.shape[-1]
    HC = x_ref.shape[2]
    HT = cot_ref.shape[2]
    HB = HC + HT
    heads = HEADS // n_mp
    pheads = PHEADS // n_mp
    wq = q_s.shape[-1]
    wpq = pq_s.shape[-1]
    FH = a_s.shape[-1]
    PF = pa_s.shape[-1]
    scale = (wq // heads) ** -0.5
    pscale = (wpq // pheads) ** -0.5
    en1, en2, pn1, pn2 = (
        ref[...].reshape(1, ref.shape[0]) for ref in (gain_e1, gain_e2, gain_p1, gain_p2)
    )

    def mp_peer(j):
        return lax.rem(r + j, n_mp)

    def mp_source(j):
        return lax.rem(r + n_mp - j, n_mp)

    def z_peer(j):
        return lax.rem(z + j, nb)

    def z_source(j):
        return lax.rem(z + nb - j, nb)

    def rows_at(block, rows):
        return pl.ds(pl.multiple_of(block * rows, rows), rows)

    def send_to(src, dst, send_sem, recv_sem, **device):
        return pltpu.make_async_remote_copy(
            src_ref=src, dst_ref=dst, send_sem=send_sem, recv_sem=recv_sem,
            device_id=device, device_id_type=MESH,
        )

    def landing(chunk):
        return xin.at[chunk], cin.at[chunk], pin.at[chunk, x]

    def local_copies(part, mb):
        chunk = y if part == 0 else 2
        sources = (x_ref.at[0, mb], cot_ref.at[0, mb], places.at[mb])
        return [
            pltpu.make_async_copy(src, dst, inl.at[part, n])
            for n, (src, dst) in enumerate(zip(sources, landing(chunk)))
        ]

    for copy in local_copies(0, base + s):
        copy.start()

    @pl.when(s == y)
    def _():
        for copy in local_copies(1, base + 2):
            copy.start()

    def own_quarter(i):
        dst = w_vmem[i] if i == 4 else w_vmem[i].at[0]
        return pltpu.make_async_copy(w_hbm[i], dst, w_sem.at[i])

    for i in range(n_weight):
        own_quarter(i).start()

    barrier = pltpu.get_barrier_semaphore()
    for j in range(1, n_mp):
        pl.semaphore_signal(barrier, inc=1, device_id={"mp": mp_peer(j)}, device_id_type=MESH)
    for j in range(1, nb):
        pl.semaphore_signal(barrier, inc=1, device_id={"batch": z_peer(j)}, device_id_type=MESH)
    pl.semaphore_signal(barrier, inc=1, device_id={"section": other}, device_id_type=MESH)
    pl.semaphore_signal(
        barrier, inc=1, device_id={"section": other, "mp": y_peer}, device_id_type=MESH
    )
    pl.semaphore_wait(barrier, n_mp - 1 + nb - 1 + 2)

    def input_copies(part, mb):
        chunk = y if part == 0 else 2
        sources = (x_ref.at[0, mb], cot_ref.at[0, mb], places.at[mb])
        return [
            send_to(src, dst, ins.at[part, n], inr.at[part, n], mp=y_peer)
            for n, (src, dst) in enumerate(zip(sources, landing(chunk)))
        ]

    def input_waits(part):
        chunk = 1 - y if part == 0 else 2
        for n, dst in enumerate(landing(chunk)):
            send_to(dst, dst, ins.at[part, n], inr.at[part, n], mp=y_peer).wait_recv()

    far = (1 - y) * nm
    for copy in input_copies(0, far + s):
        copy.start()

    @pl.when(s == y)
    def _():
        for copy in input_copies(1, far + 2):
            copy.start()

    n_parcel = 12

    def parcel(refs, n):
        if n < 3:
            return refs[0].at[n]
        if n == 3:
            return refs[1]
        if n < 8:
            ref = refs[2 + (n - 4) // 2]
            rows = ref.shape[0] // 2
            return ref.at[pl.ds((n - 4) % 2 * rows, rows)]
        return refs[n - 3]

    def share(n, ref, number, of):
        if n == 8:
            rows = ref.shape[1] // of
            return ref.at[:, rows_at(number, rows)]
        rows = ref.shape[0] // of
        return ref.at[rows_at(number, rows)]

    away = [ref if i == 4 else ref.at[1] for i, ref in enumerate(w_vmem)]

    def p_far(n):
        number, of = (s, 2) if n in DIRECT else (2 * s + pair, 4)
        return send_to(
            share(n, parcel(w_hbm, n), number, of), share(n, parcel(away, n), number, of),
            wys.at[n], wyr.at[n], mp=y_peer,
        )

    def p_pair(n, which):
        block = share(n, parcel(away, n), 2 * s + which, 4)
        return send_to(block, block, wzs.at[n], wzr.at[n], batch=z_pair)

    def p_swap(n, which):
        block = share(n, parcel(away, n), which, 2)
        return send_to(block, block, wcs.at[n], wcr.at[n], section=other)

    def fetch(*parcels):
        for n in parcels:
            p_far(n).start()

    def to_pair(*parcels):
        for n in parcels:
            p_far(n).wait_recv()
            p_pair(n, pair).start()

    def to_core(*parcels):
        for n in parcels:
            if n not in DIRECT:
                p_pair(n, 1 - pair).wait_recv()
            else:
                p_far(n).wait_recv()
            p_swap(n, s).start()

    def arrived(*parcels):
        for n in parcels:
            p_swap(n, other).wait_recv()

    def at_hand(*matrices):
        for i in matrices:
            own_quarter(i).wait()

    fetch(0, 1, 2, 3)

    def ag_send(buf, rows, ph, c):
        mine = buf.at[c, rows_at(x, rows)]
        send_to(mine, mine, ss.at[ph, c], rs.at[ph, c], mp=x_peer).start()

    def ag_wait(buf, rows, ph, c):
        theirs = buf.at[c, rows_at(1 - x, rows)]
        send_to(theirs, theirs, ss.at[ph, c], rs.at[ph, c], mp=x_peer).wait_recv()

    def rs_copy(part, rb, rows, ph, c):
        return send_to(
            part.at[c, rows_at(1 - x, rows)], rb.at[c], ss.at[ph, c], rs.at[ph, c], mp=x_peer
        )

    def rs_send(part, rb, rows, ph, c):
        rs_copy(part, rb, rows, ph, c).start()

    def own_sum(part, rb, rows, c, top, size):
        at = pl.ds(pl.multiple_of(x * rows + top, 16), size)
        return part[c, at, :].astype(F32) + rb[c, top:top + size, :].astype(F32)

    def own_tile(rows, top, size):
        return pl.ds(pl.multiple_of(x * rows + top, 16), size)

    def ex_copy(src, dst, ph, c):
        return send_to(src.at[c], dst.at[c], ss.at[ph, c], rs.at[ph, c], mp=x_peer)

    def ex_wait(src, dst, ph, c):
        ex_copy(src, dst, ph, c).wait_recv()

    def ex_sum(src, dst, c, at):
        return src[c, at, :].astype(F32) + dst[c, at, :].astype(F32)

    def pin_copy(c, block):
        at = pin.at[c, block]
        return send_to(at, at, ss.at[AG_PIN, c], rs.at[AG_PIN, c], mp=x_peer)

    def each(body, first=0):
        def step(n, carry):
            body(lax.rem(n + first, nm) if first else n)
            return carry
        lax.fori_loop(0, nm, step, 0)

    def spot(c):
        return jnp.where(c == 2, s, c), base + jnp.where(c == 2, 2, s), lax.div(c, 2)

    def minor_add(row, values):
        width = values.shape[-1]
        values = jnp.sum(values, axis=0, keepdims=True)
        minor[pl.ds(row, 1), 0:width] = minor[pl.ds(row, 1), 0:width] + values

    def wgrad(lhs, rhs, chunk, *targets):
        rows = lhs.shape[0] * lhs.shape[1]

        def step(n, carry):
            at = pl.ds(pl.multiple_of(n * chunk, chunk), chunk)
            left = lhs[:, :, at].reshape(rows, chunk).T
            for i in range(2):
                for matrix, lead, first, last in targets:
                    right = rhs[i, :, :, first:last].reshape(rows, last - first)
                    g_full[matrix][i, at, lead:lead + last - first] = mm(left, right).astype(BF16)
            return carry
        lax.fori_loop(0, lhs.shape[-1] // chunk, step, 0)

    def pieces(rows, body):
        size = rows // 4

        def step(n, carry):
            body(n, size)
            return carry
        lax.fori_loop(0, 4, step, 0)

    def half_rows(i):
        return g_full[i].shape[1] // 2

    def core_copy(i):
        return send_to(
            g_full[i].at[:, rows_at(other, half_rows(i))], g_core[i], gcs.at[i], gcr.at[i],
            section=other,
        )

    def core_start(i):
        core_copy(i).start()

    def put(i, total, at=slice(None)):
        first = (0, 2, 3, 4, 6, 7, 0, 2, 3)[i]
        if i == 0:
            for part in range(2):
                grad_out[0][part, at, :] = total[:, part * wq:(part + 1) * wq]
        elif i == 6:
            grad_out[0][2, at, :] = total[:, 0:wq]
            tail = total[:, wq:]
            grad_out[1][at, :] = tail.T if z_inside else tail
        elif i == 3:
            for part in range(3):
                grad_out[4][part, at, :] = total[:, part * wpq:(part + 1) * wpq]
            grad_out[5][at, :] = total[:, 3 * wpq:]
        elif i in (1, 2):
            grad_out[first][at, 0:FH // 2] = total
        elif i in (7, 8):
            grad_out[first][at, FH // 2:FH] = total
        else:
            grad_out[first][at, :] = total

    z_far = lax.rem(z + 2, 4)

    def z_slice(i, number):
        rows = half_rows(i) // 4
        return pl.ds(pl.multiple_of(s * half_rows(i) + number * rows, rows), rows)

    def near_copies(i):
        return [
            send_to(
                g_full[i].at[j, z_slice(i, 1 - pair + 2 * m)], g_z[i].at[2 * j + m],
                gzs.at[i, 2 * j + m], gzr.at[i, 2 * j + m], batch=z_pair,
            )
            for j in ((1, 0) if i in Z_FIRST else (0,)) for m in range(2)
        ]

    def y_copies(i):
        if not z_inside or i not in Z_FIRST:
            mine = g_full[i].at[1, rows_at(s, half_rows(i))]
            return [send_to(mine, g_y[i].at[0], gys.at[i, 0], gyr.at[i, 0], mp=y_peer)]
        return [
            send_to(
                g_full[i].at[1, z_slice(i, pair + 2 * m)], g_y[i].at[m], gys.at[i, m],
                gyr.at[i, m], mp=y_peer,
            )
            for m in range(2)
        ]

    def far_copy(i):
        return send_to(
            g_full[i].at[0, z_slice(i, z_far)], g_z[i].at[4], gzs.at[i, 4], gzr.at[i, 4],
            batch=z_far,
        )

    def add_core(i):
        core_copy(i).wait_recv()

        def piece(n, size):
            mine, at = rows_at(4 * s + n, size), rows_at(n, size)
            for j in range(2):
                g_full[i][j, mine, :] = g_full[i][j, mine, :] + g_core[i][j, at, :]

        pieces(half_rows(i), piece)

    def add_near(i):
        for copy in near_copies(i):
            copy.wait_recv()
        for j in (1, 0) if i in Z_FIRST else (0,):
            for m in range(2):
                at = z_slice(i, pair + 2 * m)
                g_full[i][j, at, :] = g_full[i][j, at, :] + g_z[i][2 * j + m]

    def add_y(i):
        for copy in y_copies(i):
            copy.wait_recv()
        if i in Z_FIRST:
            for m in range(2):
                at = z_slice(i, pair + 2 * m)
                g_full[i][0, at, :] = g_full[i][0, at, :] + g_y[i][m]
            return

        def piece(n, size):
            mine, at = rows_at(4 * s + n, size), rows_at(n, size)
            g_full[i][0, mine, :] = g_full[i][0, mine, :] + g_y[i][0, at, :]

        pieces(half_rows(i), piece)

    def near(*matrices):
        for i in matrices:
            add_core(i)
            for copy in near_copies(i) if z_inside and i in Z_FIRST else y_copies(i):
                copy.start()

    def across(*matrices):
        if not z_inside:
            return
        for i in matrices:
            if i in Z_FIRST:
                add_near(i)
            else:
                add_y(i)
            for copy in y_copies(i) if i in Z_FIRST else near_copies(i):
                copy.start()

    def onward(*matrices):
        for i in matrices:
            if not z_inside:
                for copy in y_copies(i):
                    copy.wait_recv()
                put(i, g_full[i][0, rows_at(s, half_rows(i)), :] + g_y[i][0])
                continue
            if i in Z_FIRST:
                add_y(i)
            else:
                add_near(i)
            far_copy(i).start()

    def finish(*matrices):
        if not z_inside:
            return
        for i in matrices:
            far_copy(i).wait_recv()
            put(i, g_full[i][0, z_slice(i, z), :].astype(F32) + g_z[i][4].astype(F32))

    def first_rows(c):
        for top in range(0, HC, 16):
            rows = xin[c, top:top + 16, :].astype(F32)
            h1g[c, own_tile(HC, top, 16), :] = norm_forward(rows, en1).astype(BF16)
        ag_send(h1g, HC, AG_H1, c)
        cotg[c, rows_at(x, HT), :] = cin[c]
        ag_send(cotg, HT, AG_COT, c)
        pin_copy(c, x).start()

    for copy in local_copies(0, base + s):
        copy.wait()
    minor[...] = jnp.zeros_like(minor)

    def first_step(n, carry):
        @pl.when(n == 1)
        def _():
            input_waits(0)

        @pl.when(jnp.logical_and(n == 2, s != y))
        def _():
            input_waits(1)

        @pl.when(jnp.logical_and(n == 2, s == y))
        def _():
            for copy in local_copies(1, base + 2):
                copy.wait()

        first_rows(jnp.where(n == 2, 2, jnp.where(n == 0, y, 1 - y)))
        return carry

    lax.fori_loop(0, nm, first_step, 0)

    half = PW // 2
    frequency = jnp.exp(
        lax.broadcasted_iota(jnp.int32, (1, half), 1).astype(F32)
        * (-2.0 * math.log(10000.0) / PW)
    )

    def mask_rows(c):
        pin_copy(c, 1 - x).wait_recv()
        here = lax.broadcasted_iota(jnp.int32, (HT, HT), 0)
        there = lax.broadcasted_iota(jnp.int32, (HT, HT), 1)
        for b in range(2):
            row = pin[c, b].astype(F32)
            column = jnp.sum(jnp.where(here == there, row, 0.0), axis=1, keepdims=True)
            sine, cosine = turns(column * frequency)
            at = slice(b * HT, (b + 1) * HT)
            m_s[c, at, 0:half] = sine
            m_s[c, at, half:PW] = cosine
        for b in range(2):
            at = slice(b * HT, (b + 1) * HT)
            rows = m_s[c, at, :] + mask_token[...].reshape(1, PW)
            m_s[c, at, :] = rows
            normed = norm_forward(rows, pn1).astype(BF16)
            pt1[c, at, :] = normed
            ph1g[c, b * HB + HC:(b + 1) * HB, :] = normed

    n_row = 2 * HC
    n_ctx = n_mp * HC

    def kv_copy(buf, slot, which, i=slice(None)):
        rows = buf.shape[3] // 2
        block = buf.at[1, i, :, rows_at(which, rows)]
        return send_to(block, block, kvs.at[slot], kvr.at[slot], section=other)

    def stack(values, n_heads):
        width = values.shape[-1]
        return jnp.concatenate(
            [values * head_mask(width, width // n_heads, h) for h in range(n_heads)], axis=0
        )

    def unstack(values, n_heads):
        rows, width = values.shape[0] // n_heads, values.shape[-1]
        lane = lax.broadcasted_iota(jnp.int32, (1, width), 1)
        out = values[(n_heads - 1) * rows:]
        for h in range(n_heads - 2, -1, -1):
            out = jnp.where(lane < (h + 1) * (width // n_heads), values[h * rows:(h + 1) * rows], out)
        return out

    tile = 32

    def attend(q, k, v, bias, scaling, n_heads, p_ref):
        rows = q.shape[0]
        scores = mm_nt(stack(q, n_heads), k)
        for at in range(0, n_heads * rows, tile):
            low = at % rows
            t = scores[at:at + tile] * (scaling * LOG2E) + bias[low:low + tile]
            e = jnp.exp2(t - jnp.max(t, axis=-1, keepdims=True))
            p = e * reciprocal(jnp.sum(e, axis=-1, keepdims=True))
            p_ref[at:at + tile, :] = p.astype(BF16)
        return unstack(mm(p_ref[...], v), n_heads).astype(BF16)

    def attend_back(q, k, v, o, do, scaling, n_heads, p_ref, ds_ref):
        rows = q.shape[0]
        do_all = stack(do, n_heads)
        o_all = jnp.concatenate([o] * n_heads, axis=0)
        dp = mm_nt(do_all, v)
        for at in range(0, n_heads * rows, tile):
            part = slice(at, at + tile)
            delta = jnp.sum(
                do_all[part].astype(F32) * o_all[part].astype(F32), axis=-1, keepdims=True
            )
            ds_ref[part, :] = (p_ref[part, :].astype(F32) * (dp[part] - delta)).astype(BF16)
        ds = ds_ref[0:n_heads * rows, :]
        dq = unstack(mm(ds, k), n_heads)
        dk = mm_tn(ds, stack(q, n_heads))
        dv = mm_tn(p_ref[...], do_all)
        return dq * scaling, dk * scaling, dv

    def enc_qkv(c, i):
        place, _, keys = spot(c)
        if i == 0:
            ag_wait(h1g, HC, AG_H1, c)
        h1 = h1g[c]
        q_s[i, c] = mm_nt(h1, eqkv[i, 0]).astype(BF16)
        kv_s[keys, i, 0, rows_at(place, n_row), :] = mm_nt(h1, eqkv[i, 1]).astype(BF16)
        kv_s[keys, i, 1, rows_at(place, n_row), :] = mm_nt(h1, eqkv[i, 2]).astype(BF16)

        @pl.when(c == 2)
        def _():
            kv_copy(kv_s, i, s, i).start()

    def members(which):
        return slice(0, 2) if which == 0 else slice(2, 3)

    def half_of(which):
        return (base + s, 0) if which == 0 else (base + 2, s)

    def join(values):
        return values.reshape(values.shape[0] * values.shape[1], values.shape[2])

    def enc_attention(which, i):
        own = members(which)
        mb, place = half_of(which)
        if which == 1:
            kv_copy(kv_s, i, other, i).wait_recv()
        rows = (2 - which) * n_row
        ends = bounds_of(ctx_len, mb)
        qs = segment(lax.broadcasted_iota(jnp.int32, (rows, 1), 0) + place * n_row, ends)
        ks = segment(lax.broadcasted_iota(jnp.int32, (1, n_ctx), 1), ends)
        bias = jnp.where(qs == ks, 0.0, -1e30).astype(F32)
        o = attend(
            join(q_s[i, own]), kv_s[which, i, 0], kv_s[which, i, 1], bias, scale, heads,
            (p_a, p_b)[which].at[i],
        )
        o_s[i, own] = o.reshape(2 - which, n_row, wq)
        if i == 1:
            out = mm(join(o_s[0, own]), eproj[0]) + mm(o, eproj[1])
            part[own] = out.astype(BF16).reshape(2 - which, n_row, W)
            for c in range(own.start, own.stop):
                rs_send(part, rb_o, HC, RS_O, c)

    def enc_second_norm(c):
        rs_copy(part, rb_o, HC, RS_O, c).wait_recv()
        for top in range(0, HC, 16):
            x1 = xin[c, top:top + 16, :].astype(F32) + own_sum(part, rb_o, HC, c, top, 16)
            x1_s[c, top:top + 16, :] = x1
            h2g[c, own_tile(HC, top, 16), :] = norm_forward(x1, en2).astype(BF16)
        ag_send(h2g, HC, AG_H2, c)

    def gelu_tiles(h, weight, a_ref, slope_ref):
        for left in range(0, weight.shape[1], 256):
            right = min(left + 256, weight.shape[1])
            u = mm(h, weight[:, left:right])
            for top in range(0, h.shape[0], 16):
                a, slope = gelu_parts(u[top:top + 16])
                a_ref[top:top + 16, left:right] = a.astype(BF16)
                slope_ref[top:top + 16, left:right] = slope.astype(BF16)

    def slope_tiles(da, weight, slope_ref):
        for left in range(0, weight.shape[0], 256):
            right = min(left + 256, weight.shape[0])
            back = mm_nt(da, weight[left:right, :])
            for top in range(0, da.shape[0], 32):
                at = (slice(top, top + 32), slice(left, right))
                slope_ref[at] = (back[top:top + 32] * slope_ref[at].astype(F32)).astype(BF16)

    def enc_mlp(c, i):
        if i == 0:
            ag_wait(h2g, HC, AG_H2, c)
            rs_copy(part, rb_o, HC, RS_O, c).wait_send()
        gelu_tiles(h2g[c], eup[i], a_s.at[i, c], gp_s.at[i, c])
        total = mm(a_s[i, c], edown[i])
        if i == 1:
            total = total + part[c].astype(F32)
        part[c] = total.astype(BF16)
        if i == 1:
            rs_send(part, rb_a, HC, RS_A, c)

    def p1_copy(c, block):
        at = ph1g.at[c, pl.ds(pl.multiple_of(block * HB, 16), HC)]
        return send_to(at, at, ss.at[AG_P1, c], rs.at[AG_P1, c], mp=x_peer)

    def link_forward(c):
        rs_copy(part, rb_a, HC, RS_A, c).wait_recv()
        for top in range(0, HC, 16):
            out = x1_s[c, top:top + 16, :] + own_sum(part, rb_a, HC, c, top, 16)
            y_s[c, top:top + 16, :] = out.astype(BF16)
        z_s[c] = mm(y_s[c], link[...])
        for top in range(0, HC, 32):
            rows = norm_forward(z_s[c, top:top + 32, :], pn1)
            at = pl.ds(pl.multiple_of(x * HB + top, 16), 32)
            ph1g[c, at, :] = rows.astype(BF16)
        p1_copy(c, x).start()

    def own_first(body, i):
        each(lambda c: body(c, i))

    for n in range(4):
        to_pair(n)
        fetch(n + 4)
    at_hand(0, 1)
    own_first(enc_qkv, 0)
    to_core(0, 1, 2, 3)
    to_pair(4)
    enc_attention(0, 0)
    to_pair(5)
    enc_attention(1, 0)
    each(mask_rows)
    arrived(0, 1, 2)
    own_first(enc_qkv, 1)
    to_core(4)
    to_pair(6)
    arrived(3)
    enc_attention(0, 1)
    to_core(5)
    to_pair(7)
    enc_attention(1, 1)
    fetch(8, 9, 10, 11)

    def second_norm_step(c):
        enc_second_norm(c)

        @pl.when(c == 0)
        def _():
            to_core(6)

        @pl.when(c == 2)
        def _():
            to_core(7)

    each(second_norm_step)
    at_hand(2, 3)
    own_first(enc_mlp, 0)
    arrived(4, 5, 6, 7)
    to_pair(10, 11)
    own_first(enc_mlp, 1)
    to_core(8, 9, 10, 11)
    at_hand(4)
    each(link_forward)

    n_blk = 2 * HB
    n_all = n_mp * HB
    n_tgt = 2 * HT

    def pred_qkv(c):
        place, _, keys = spot(c)
        p1_copy(c, 1 - x).wait_recv()
        h1 = ph1g[c]
        for i in range(2):
            pq_s[i, c] = mm_nt(pt1[c], pqkv[i, 0]).astype(BF16)
            pkv_s[keys, i, 0, rows_at(place, n_blk), :] = mm_nt(h1, pqkv[i, 1]).astype(BF16)
            pkv_s[keys, i, 1, rows_at(place, n_blk), :] = mm_nt(h1, pqkv[i, 2]).astype(BF16)

        @pl.when(c == 2)
        def _():
            kv_copy(pkv_s, 2, s).start()

    def quarters(body):
        def step(i, carry):
            body(i)
            return carry
        lax.fori_loop(0, 2, step, 0)

    def pred_attention(which):
        own = members(which)
        mb, place = half_of(which)
        if which == 1:
            kv_copy(pkv_s, 2, other).wait_recv()
        rows = (2 - which) * n_tgt
        c_ends = bounds_of(ctx_len, mb)
        t_ends = bounds_of(tgt_len, mb)
        qs = segment(lax.broadcasted_iota(jnp.int32, (rows, 1), 0) + place * n_tgt, t_ends)
        row = lax.broadcasted_iota(jnp.int32, (1, n_all), 1)
        block = jnp.zeros((1, n_all), jnp.int32)
        for b in range(1, n_mp):
            block = block + jnp.where(row >= b * HB, 1, 0)
        inner = row - block * HB
        c_seg = segment(block * HC + inner, c_ends)
        t_seg = segment(block * HT + inner - HC, t_ends)
        ks = jnp.where(inner < HC, c_seg, t_seg)
        bias = jnp.where(qs == ks, 0.0, -1e30).astype(F32)
        for i in range(2):
            o = attend(
                join(pq_s[i, own]), pkv_s[which, i, 0], pkv_s[which, i, 1], bias, pscale, pheads,
                (pp_a, pp_b)[which].at[i],
            )
            po_s[i, own] = o.reshape(2 - which, n_tgt, wpq)
        out = mm(join(po_s[0, own]), pproj[0]) + mm(join(po_s[1, own]), pproj[1])
        part_p[own] = out.astype(BF16).reshape(2 - which, n_tgt, PW)
        for c in range(own.start, own.stop):
            ex_copy(part_p, rb_po, RS_PO, c).start()

    def pred_mlp(c):
        ex_wait(part_p, rb_po, RS_PO, c)
        for top in range(0, n_tgt, 32):
            at = slice(top, top + 32)
            x1 = m_s[c, at, :] + ex_sum(part_p, rb_po, c, at)
            px1_s[c, at, :] = x1
            ph2g[c, at, :] = norm_forward(x1, pn2).astype(BF16)
        ag_wait(cotg, HT, AG_COT, c)
        total = jnp.zeros((n_tgt, PW), F32)
        for i in range(2):
            gelu_tiles(ph2g[c], pup[i], pa_s.at[i, c], pdu_s.at[i, c])
            slope_tiles(cotg[c], pdown[i], pdu_s.at[i, c])
            total = total + mm_nt(pdu_s[i, c], pup[i])
        ex_copy(part_p, rb_po, RS_PO, c).wait_send()
        part_p[c] = total.astype(BF16)
        ex_copy(part_p, rb_p2, RS_P2, c).start()

    def dkv_copy(slot, outgoing, incoming):
        return send_to(outgoing, incoming, kvs.at[slot], kvr.at[slot], section=other)

    def pred_second_back(c):
        ex_wait(part_p, rb_p2, RS_P2, c)
        for block in range(2):
            counted = jnp.where(x == block, 1.0, 0.0).astype(F32)
            at = slice(block * HT, (block + 1) * HT)
            dxn, dgain = norm_backward(px1_s[c, at, :], pn2, ex_sum(part_p, rb_p2, c, at))
            dx1 = cotg[c, at, :].astype(F32) + dxn
            pdbg[c, at, :] = dx1.astype(BF16)
            minor_add(3, fold(dgain) * counted)
            minor_add(4, fold(dx1) * counted)

    def pred_attention_back(which):
        own = members(which)
        for c in range(own.start, own.stop):
            pred_second_back(c)

        def one(i):
            do = mm_nt(join(pdbg[own]), pproj[i]).astype(BF16)
            dq, dk, dv = attend_back(
                join(pq_s[i, own]), pkv_s[which, i, 0], pkv_s[which, i, 1], join(po_s[i, own]),
                do, pscale, pheads, (pp_a, pp_b)[which].at[i], pds_s,
            )
            pdq_s[i, own] = dq.astype(BF16).reshape(2 - which, n_tgt, wpq)
            if which == 0:
                pdkv_s[i, own, :, 0:wpq] = dk.astype(BF16).reshape(2, n_blk, wpq)
                pdkv_s[i, own, :, wpq:2 * wpq] = dv.astype(BF16).reshape(2, n_blk, wpq)
            else:
                pdkv_acc[i, 0] = dk
                pdkv_acc[i, 1] = dv

        quarters(one)
        if which == 1:
            pdkv_x[...] = pdkv_acc[:, :, rows_at(other, n_blk), :].astype(BF16)
            dkv_copy(3, pdkv_x, pdkv_r).start()

    def pred_rows_back(c):
        @pl.when(c == 2)
        def _():
            dkv_copy(3, pdkv_x, pdkv_r).wait_recv()
            for i in range(2):
                for which in range(2):
                    total = pdkv_acc[i, which, rows_at(s, n_blk), :] + pdkv_r[i, which].astype(F32)
                    pdkv_s[i, 2, :, which * wpq:(which + 1) * wpq] = total.astype(BF16)

        from_q = jnp.zeros((n_tgt, PW), F32)
        from_kv = jnp.zeros((n_blk, PW), F32)
        for i in range(2):
            from_q = from_q + mm(pdq_s[i, c], pqkv[i, 0])
            from_kv = from_kv + mm(pdkv_s[i, c, :, 0:wpq], pqkv[i, 1])
            from_kv = from_kv + mm(pdkv_s[i, c, :, wpq:2 * wpq], pqkv[i, 2])
        for b in range(2):
            part_p1[c, b * HC:(b + 1) * HC, :] = from_kv[b * HB:b * HB + HC].astype(BF16)
        rs_send(part_p1, rb_p1, HC, RS_P1, c)
        for b in range(2):
            dh1 = from_kv[b * HB + HC:(b + 1) * HB] + from_q[b * HT:(b + 1) * HT]
            dz, dgain = norm_backward(m_s[c, b * HT:(b + 1) * HT, :], pn1, dh1)
            minor_add(2, fold(dgain))
            minor_add(4, fold(dz))

    def pred_first_back(c):
        rs_copy(part_p1, rb_p1, HC, RS_P1, c).wait_recv()
        gain_sum = jnp.zeros((8, PW), F32)
        for top in range(0, HC, 32):
            dh1 = own_sum(part_p1, rb_p1, HC, c, top, 32)
            dz, dgain = norm_backward(z_s[c, top:top + 32, :], pn1, dh1)
            gain_sum = gain_sum + fold(dgain)
            dcg[c, own_tile(HC, top, 32), :] = dz.astype(BF16)
        minor_add(2, gain_sum)
        ag_send(dcg, HC, AG_DY, c)

    at_hand(5, 6, 7, 8)
    arrived(8, 9, 10, 11)
    each(pred_qkv)
    pred_attention(0)
    pred_attention(1)
    each(pred_mlp)
    wgrad(ph2g, pdu_s, 128, (4, 0, 0, PF))
    core_start(4)
    wgrad(cotg, pa_s, 128, (5, 0, 0, PF))
    core_start(5)
    pred_attention_back(1)
    pred_attention_back(0)
    each(pred_rows_back)
    near(4, 5)
    wgrad(pdbg, po_s, 128, (3, 3 * wpq, 0, wpq))
    wgrad(pt1, pdq_s, 128, (3, 0, 0, wpq))
    wgrad(ph1g, pdkv_s, 128, (3, wpq, 0, 2 * wpq))
    core_start(3)
    each(pred_first_back)
    across(4, 5)
    near(3)

    l_right = dcg[:, rows_at(x, HC), :].reshape(nm * HC, PW)

    def link_step(n, carry):
        at = pl.ds(pl.multiple_of(n * 256, 256), 256)
        l_full[at, :] = mm_tn(y_s[:, :, at].reshape(nm * HC, 256), l_right).astype(BF16)
        return carry

    lax.fori_loop(0, W // 256, link_step, 0)
    lh = l_full.shape[0] // 2
    lq = lh // n_mp
    l_core_copy = send_to(
        l_full.at[rows_at(other, lh)], l_core, lcs.at[0], lcr.at[0], section=other
    )
    l_core_copy.start()

    def l_mp_copy(j):
        return send_to(
            l_half.at[rows_at(mp_peer(j), lq)], l_mp.at[j - 1], lms.at[j - 1], lmr.at[j - 1],
            mp=mp_peer(j),
        )

    def l_z_copy(j, slot):
        return send_to(
            l_z.at[slot], l_z.at[slot], lzs.at[j - 1], lzr.at[j - 1], batch=z_peer(j)
        )

    def l_all_copy(j, block):
        at = l_all.at[pl.ds(pl.multiple_of(s * lh + block * lq, lq), lq)]
        return send_to(at, at, las.at[j - 1], lar.at[j - 1], mp=mp_peer(j))

    def l_back_copy(block):
        at = l_all.at[rows_at(block, lh)]
        return send_to(at, at, lcs.at[1], lcr.at[1], section=other)

    def form_dy(c):
        ag_wait(dcg, HC, AG_DY, c)
        dyg[c] = mm_nt(dcg[c], link[...]).astype(BF16)

    def enc_mlp_back(c):
        dy = dyg[c]
        total = jnp.zeros((n_row, W), F32)
        for i in range(2):
            slope_tiles(dy, edown[i], gp_s.at[i, c])
            total = total + mm_nt(gp_s[i, c], eup[i])
        rs_copy(part, rb_a, HC, RS_A, c).wait_send()
        part[c] = total.astype(BF16)
        rs_send(part, rb_2, HC, RS_2, c)

    def enc_second_back(c):
        rs_copy(part, rb_2, HC, RS_2, c).wait_recv()
        gain_sum = jnp.zeros((8, W), F32)
        for top in range(0, HC, 16):
            at = slice(top, top + 16)
            dh2 = own_sum(part, rb_2, HC, c, top, 16)
            dxn, dgain = norm_backward(x1_s[c, at, :], en2, dh2)
            gain_sum = gain_sum + fold(dgain)
            dx1 = dyg[c, own_tile(HC, top, 16), :].astype(F32) + dxn
            dx1_s[c, at, :] = dx1
            dbg[c, own_tile(HC, top, 16), :] = dx1.astype(BF16)
        minor_add(1, gain_sum)
        ag_send(dbg, HC, AG_B, c)

    def enc_attention_back(which):
        own = members(which)
        for c in range(own.start, own.stop):
            ag_wait(dbg, HC, AG_B, c)

        def one(i):
            do = mm_nt(join(dbg[own]), eproj[i]).astype(BF16)
            dq, dk, dv = attend_back(
                join(q_s[i, own]), kv_s[which, i, 0], kv_s[which, i, 1], join(o_s[i, own]), do,
                scale, heads, (p_a, p_b)[which].at[i], ds_s,
            )
            dqkv_s[i, own, :, 0:wq] = dq.astype(BF16).reshape(2 - which, n_row, wq)
            if which == 0:
                dqkv_s[i, own, :, wq:2 * wq] = dk.astype(BF16).reshape(2, n_row, wq)
                dqkv_s[i, own, :, 2 * wq:3 * wq] = dv.astype(BF16).reshape(2, n_row, wq)
            else:
                dkv_acc[i, 0] = dk
                dkv_acc[i, 1] = dv

        quarters(one)
        if which == 1:
            dkv_x[...] = dkv_acc[:, :, rows_at(other, n_row), :].astype(BF16)
            dkv_copy(4, dkv_x, dkv_r).start()

    def enc_shared_keys():
        dkv_copy(4, dkv_x, dkv_r).wait_recv()
        for i in range(2):
            for which in range(2):
                total = dkv_acc[i, which, rows_at(s, n_row), :] + dkv_r[i, which].astype(F32)
                dqkv_s[i, 2, :, (which + 1) * wq:(which + 2) * wq] = total.astype(BF16)

    def enc_rows_back(c):
        total = jnp.zeros((n_row, W), F32)
        for i in range(2):
            for which in range(3):
                total = total + mm(dqkv_s[i, c, :, which * wq:(which + 1) * wq], eqkv[i, which])
        rs_copy(part, rb_2, HC, RS_2, c).wait_send()
        part[c] = total.astype(BF16)
        rs_send(part, rb_1, HC, RS_1, c)

    def dx_same(chunk, slot):
        return send_to(dx_s.at[chunk], dx_r.at[slot], dxs.at[0], dxr.at[slot], section=other)

    def dx_far(chunk, slot, sem):
        return send_to(
            dx_s.at[chunk], dx_r.at[slot], dxs.at[sem], dxr.at[slot], section=y, mp=y_peer
        )

    def enc_first_back(c):
        rs_copy(part, rb_1, HC, RS_1, c).wait_recv()
        gain_sum = jnp.zeros((8, W), F32)
        for top in range(0, HC, 16):
            at = slice(top, top + 16)
            dh1 = own_sum(part, rb_1, HC, c, top, 16)
            dxn, dgain = norm_backward(xin[c, at, :].astype(F32), en1, dh1)
            gain_sum = gain_sum + fold(dgain)
            dx1_s[c, at, :] = dx1_s[c, at, :] + dxn
            dx_s[c, at, :] = dx1_s[c, at, :].astype(BF16)
        minor_add(0, gain_sum)

        @pl.when(jnp.logical_and(s == y, c != 1 - y))
        def _():
            dx_out[0, jnp.where(c == 2, 2, s)] = dx1_s[c]

    def dx_send():
        dx_far(1 - y, s, 1).start()

        @pl.when(s != y)
        def _():
            dx_same(y, s).start()
            dx_far(2, 2, 2).start()

    each(form_dy)
    wgrad(dyg, a_s, 256, (2, 0, 0, FH // 2), (8, 0, FH // 2, FH))
    core_start(2)
    core_start(8)

    def mlp_back_step(c):
        enc_mlp_back(c)

        @pl.when(c == 2)
        def _():
            near(2, 8)
            across(3)

    each(mlp_back_step)
    l_core_copy.wait_recv()

    def l_piece(n, size):
        mine, at = rows_at(4 * s + n, size), rows_at(n, size)
        l_half[at, :] = (l_full[mine, :].astype(F32) + l_core[at, :].astype(F32)).astype(BF16)

    pieces(lh, l_piece)
    for j in range(1, n_mp):
        l_mp_copy(j).start()
    wgrad(h2g, gp_s, 256, (1, 0, 0, FH // 2), (7, 0, FH // 2, FH))
    core_start(1)
    core_start(7)
    each(enc_second_back, 2)
    onward(4, 5)
    total = l_half[rows_at(r, lq), :].astype(F32)
    for j in range(1, n_mp):
        l_mp_copy(j).wait_recv()
        total = total + l_mp[j - 1].astype(F32)
    l_z[z] = total.astype(BF16)
    for j in range(1, nb):
        l_z_copy(j, z).start()
    enc_attention_back(1)
    near(1, 7)
    enc_attention_back(0)
    enc_shared_keys()
    wgrad(dbg, o_s, 256, (6, wq, 0, wq))
    wgrad(h1g, dqkv_s, 256, (6, 0, 2 * wq, 3 * wq))
    core_start(6)
    wgrad(h1g, dqkv_s, 256, (0, 0, 0, 2 * wq))
    core_start(0)
    across(2, 8)
    onward(3)
    for j in range(1, nb):
        l_z_copy(j, z_source(j)).wait_recv()
    total = l_z[0].astype(F32)
    for j in range(1, nb):
        total = total + l_z[j].astype(F32)
    l_all[pl.ds(pl.multiple_of(s * lh + r * lq, lq), lq), :] = total.astype(BF16)
    for j in range(1, n_mp):
        l_all_copy(j, r).start()

    def rows_back_step(c):
        enc_rows_back(c)

        @pl.when(c == 0)
        def _():
            near(6)

        @pl.when(c == 1)
        def _():
            near(0)

    each(rows_back_step)
    each(enc_first_back)

    m_core_copy = send_to(minor, m_core, mcs.at[0], mcr.at[0], section=other)
    m_core_copy.start()

    def m_mp_copy(j, slot):
        return send_to(
            m_mp.at[slot], m_mp.at[slot], mms.at[j - 1], mmr.at[j - 1], mp=mp_peer(j)
        )

    def m_z_copy(j, slot):
        return send_to(
            m_z.at[slot], m_z.at[slot], mzs.at[j - 1], mzr.at[j - 1], batch=z_peer(j)
        )

    across(1, 7)
    onward(2, 8)
    for j in range(1, n_mp):
        l_all_copy(j, mp_source(j)).wait_recv()
    l_back_copy(s).start()
    across(6)
    dx_send()
    onward(1)
    m_core_copy.wait_recv()
    m_mp[r] = minor[...] + m_core[...]
    for j in range(1, n_mp):
        m_mp_copy(j, r).start()
    across(0)
    onward(7)
    for j in range(1, n_mp):
        m_mp_copy(j, mp_source(j)).wait_recv()
    total = m_mp[0]
    for j in range(1, n_mp):
        total = total + m_mp[j]
    m_z[z] = total
    for j in range(1, nb):
        m_z_copy(j, z).start()
    finish(4, 5, 3, 2, 8)
    onward(6)

    def sent(c):
        for buf, rows, ph in (
            (h1g, HC, AG_H1), (h2g, HC, AG_H2), (cotg, HT, AG_COT),
            (dcg, HC, AG_DY), (dbg, HC, AG_B),
        ):
            mine = buf.at[c, rows_at(x, rows)]
            send_to(mine, mine, ss.at[ph, c], rs.at[ph, c], mp=x_peer).wait_send()
        for buf, rb, rows, ph in (
            (part_p1, rb_p1, HC, RS_P1), (part, rb_1, HC, RS_1),
        ):
            rs_copy(buf, rb, rows, ph, c).wait_send()

    each(sent)
    each(lambda c: ex_copy(part_p, rb_p2, RS_P2, c).wait_send())
    each(lambda c: pin_copy(c, x).wait_send())
    each(lambda c: p1_copy(c, x).wait_send())
    for copy in input_copies(0, far + s):
        copy.wait_send()

    @pl.when(s == y)
    def _():
        for copy in input_copies(1, far + 2):
            copy.wait_send()

    dx_far(1 - y, s, 1).wait_send()

    @pl.when(s != y)
    def _():
        dx_same(y, s).wait_send()
        dx_far(2, 2, 2).wait_send()

    for n in range(n_parcel):
        p_far(n).wait_send()
        if n not in DIRECT:
            p_pair(n, pair).wait_send()
        p_swap(n, s).wait_send()
    for i in range(2):
        kv_copy(kv_s, i, s, i).wait_send()
    kv_copy(pkv_s, 2, s).wait_send()
    dkv_copy(3, pdkv_x, pdkv_r).wait_send()
    dkv_copy(4, dkv_x, dkv_r).wait_send()
    l_core_copy.wait_send()
    l_back_copy(s).wait_send()
    m_core_copy.wait_send()
    for j in range(1, n_mp):
        l_mp_copy(j).wait_send()
        l_all_copy(j, r).wait_send()
        m_mp_copy(j, r).wait_send()
    for j in range(1, nb):
        l_z_copy(j, z).wait_send()
        m_z_copy(j, z).wait_send()

    onward(0)
    l_back_copy(other).wait_recv()
    for j in range(1, nb):
        m_z_copy(j, z_source(j)).wait_recv()
    total = m_z[0]
    for j in range(1, nb):
        total = total + m_z[j]
    for i, row in enumerate((0, 1, 4, 2, 3)):
        width = minor_out[i].shape[0]
        minor_out[i][...] = total[row:row + 1, 0:width].reshape(width)

    @pl.when(s == y)
    def _():
        dx_same(y, other).wait_recv()
        dx_out[0, other] = dx_r[other].astype(F32)

    @pl.when(s != y)
    def _():
        for slot in range(3):
            dx_far(1, slot, 1).wait_recv()
            dx_out[0, slot] = dx_r[slot].astype(F32)

    finish(1, 7)

    def grads_sent(*matrices):
        for i in matrices:
            core_copy(i).wait_send()
            for copy in y_copies(i):
                copy.wait_send()
            if z_inside:
                for copy in near_copies(i):
                    copy.wait_send()
                far_copy(i).wait_send()

    grads_sent(1, 2, 3, 4, 5, 7, 8)
    finish(6, 0)
    grads_sent(6, 0)


def hand_over(*refs):
    count = len(refs) // 2
    for src, dst in zip(refs[:count], refs[count:]):
        dst[...] = src[...].astype(dst.dtype)


def body(
    n_mp, nb,
    encoder_in, context_lengths, target_lengths, target_places,
    encoder_norm1, encoder_qkv, encoder_proj, encoder_norm2, encoder_up, encoder_down,
    link_weight, mask_token,
    predictor_norm1, predictor_qkv, predictor_proj, predictor_norm2, predictor_up, predictor_down,
    cotangent,
):
    mb_all, HC, W = encoder_in.shape[1:]
    HT, PW = cotangent.shape[2:]
    HB = HC + HT
    nm = mb_all // 2
    C, T = n_mp * HC, n_mp * HT
    B = n_mp * HB
    wq = encoder_qkv.shape[-1]
    pq = predictor_qkv.shape[-1]
    FH = encoder_up.shape[-1]
    PF = predictor_up.shape[-1]
    heads, pheads = HEADS // n_mp, PHEADS // n_mp
    z_inside = nb == 4 and W // 2 % (16 * nb) == 0 and PW // 2 % (16 * nb) == 0

    g_shapes = [
        (W, 2 * wq), (W, FH // 2), (W, FH // 2), (PW, 4 * pq), (PW, PF), (PW, PF), (W, 2 * wq),
        (W, FH // 2), (W, FH // 2),
    ]
    parts = 2 * nb if z_inside else 2
    a, b = W // parts, PW // parts
    g_outs = [
        (3, a, wq), (wq, a) if z_inside else (a, wq), (a, FH), (a, FH),
        (3, b, pq), (b, pq), (b, PF), (b, PF),
    ]

    def vm(shape, dtype=BF16):
        return pltpu.VMEM(shape, dtype)

    def dma(*shape):
        return pltpu.SemaphoreType.DMA(shape)

    out_shape = (
        [jax.ShapeDtypeStruct((1, nm, HC, W), F32)]
        + [jax.ShapeDtypeStruct(g, F32 if z_inside else BF16) for g in g_outs]
        + [jax.ShapeDtypeStruct((W, PW), BF16)]
        + [jax.ShapeDtypeStruct((width,), F32) for width in (W, W, PW, PW, PW)]
    )
    peers = n_mp - 1
    R, T2, B2 = 2 * HC, 2 * HT, 2 * HB
    acts = [
        vm((nm, HC, W)), vm((nm, HT, PW)), vm((nm, 2, 1, HT), jnp.int32),
        vm((nm, R, W)), vm((2, nm, R, wq)), vm((2, 2, 2, C, wq)), vm((2, nm, R, wq)),
        vm((2, heads * 2 * R, C)), vm((2, heads * R, C)), vm((nm, R, W)), vm((nm, HC, W)), vm((nm, HC, W), F32),
        vm((nm, R, W)), vm((2, nm, R, FH)), vm((2, nm, R, FH)), vm((nm, HC, W)),
        vm((nm, HC, W)), vm((nm, HC, PW), F32), vm((nm, B2, PW)), vm((nm, T2, PW)),
        vm((2, nm, T2, pq)), vm((2, 2, 2, B, pq)), vm((2, nm, T2, pq)),
        vm((2, pheads * 2 * T2, B)), vm((2, pheads * T2, B)), vm((nm, T2, PW)), vm((nm, T2, PW)), vm((nm, T2, PW), F32), vm((nm, T2, PW), F32),
        vm((nm, T2, PW)), vm((2, nm, T2, PF)), vm((nm, T2, PW)), vm((2, nm, T2, PF)),
        vm((nm, T2, PW)), vm((nm, T2, PW)),
        vm((2, nm, T2, pq)), vm((2, nm, B2, 2 * pq)), vm((2, 2, B, pq), F32),
        vm((2, 2, B2, pq)), vm((2, 2, B2, pq)), vm((nm, R, PW)), vm((nm, HC, PW)),
        vm((nm, R, PW)), vm((nm, R, W)), vm((nm, HC, W)),
        vm((nm, HC, W), F32), vm((nm, R, W)), vm((2, nm, R, 3 * wq)), vm((2, 2, C, wq), F32),
        vm((2, 2, R, wq)), vm((2, 2, R, wq)), vm((nm, HC, W)),
        vm((nm, HC, W)), vm((nm, HC, W)), vm((heads * 2 * R, C)), vm((pheads * 2 * T2, B)),
    ]
    assert len(acts) == N_ACT
    weights = [
        jnp.transpose(encoder_qkv, (0, 2, 1)), encoder_proj, encoder_up, encoder_down, link_weight,
        jnp.transpose(predictor_qkv, (0, 2, 1)), predictor_proj, predictor_up, predictor_down,
    ]
    n_weight = len(weights)
    scratch = [vm(w.shape if i == 4 else (2,) + w.shape) for i, w in enumerate(weights)]
    scratch += [dma(n_weight)] + [dma(12)] * 6
    scratch += acts
    scratch += [vm((2, a, b)) for a, b in g_shapes]
    scratch += [vm((2, a // 2, b)) for a, b in g_shapes]
    scratch += [
        vm((2, a // 8, b) if z_inside and i in Z_FIRST else (1, a // 2, b))
        for i, (a, b) in enumerate(g_shapes)
    ]
    scratch += [vm((5, a // 8, b) if z_inside else (1, 16, 128)) for a, b in g_shapes]
    lq = W // 2 // n_mp
    scratch += [
        vm((W, PW)), vm((W // 2, PW)), vm((W // 2, PW)), vm((peers, lq, PW)),
        vm((nb, lq, PW)),
        vm((8, W), F32), vm((8, W), F32), vm((n_mp, 8, W), F32), vm((nb, 8, W), F32),
        dma(N_PHASE, nm), dma(N_PHASE, nm), dma(2, 3), dma(2, 3), dma(2, 3), dma(5), dma(5), dma(3), dma(3),
        dma(9), dma(9), dma(9, 2), dma(9, 2), dma(9, 5), dma(9, 5),
        dma(2), dma(2), dma(peers), dma(peers), dma(nb - 1), dma(nb - 1), dma(peers), dma(peers),
        dma(1), dma(1), dma(peers), dma(peers), dma(nb - 1), dma(nb - 1),
    ]
    in_vmem = pl.BlockSpec(memory_space=pltpu.VMEM)
    anywhere = pl.BlockSpec(memory_space=pl.ANY)
    outs = pl.pallas_call(
        functools.partial(mega, nb, z_inside),
        out_shape=out_shape,
        in_specs=[in_vmem] * 2 + [anywhere] * 3 + [in_vmem] * 5 + [anywhere] * len(weights),
        out_specs=[in_vmem] * len(out_shape),
        scratch_shapes=scratch,
        compiler_params=pltpu.CompilerParams(
            collective_id=0, has_side_effects=True, vmem_limit_bytes=62 * 1024 * 1024
        ),
    )(
        jnp.transpose(context_lengths, (0, 2, 1)),
        jnp.transpose(target_lengths, (0, 2, 1)),
        jnp.transpose(target_places, (1, 0, 2)),
        encoder_in, cotangent,
        encoder_norm1, encoder_norm2, mask_token, predictor_norm1, predictor_norm2,
        *weights,
    )
    if z_inside:
        outs = pl.pallas_call(
            hand_over,
            out_shape=[jax.ShapeDtypeStruct(o.shape, F32) for o in out_shape],
            in_specs=[in_vmem] * len(out_shape),
            out_specs=[in_vmem] * len(out_shape),
        )(*outs)
        grads = outs[1:9]
        eproj = grads[1]
    else:
        outs = [o.astype(F32) for o in outs]
        grads = [
            lax.psum_scatter(g, "batch", scatter_dimension=g.ndim - 2, tiled=True)
            for g in outs[1:9]
        ]
        eproj = grads[1].T
    dx, link_grad = outs[0], outs[9]
    e1, e2, mask_grad, p1, p2 = outs[10:]
    return (
        dx, e1, grads[0], eproj, e2, grads[2], grads[3].T, link_grad, mask_grad,
        p1, grads[4], grads[5].T, p2, grads[6], grads[7].T,
    )


def solution(mesh):
    return jax.shard_map(
        functools.partial(body, mesh.shape["mp"], mesh.shape["batch"]),
        mesh=mesh,
        in_specs=(
            P("batch", None, "mp", None),
            P("batch", None, None),
            P("batch", None, None),
            P("batch", None, "mp"),
            P(),
            P(None, None, "mp"),
            P("mp", None),
            P(),
            P(None, "mp"),
            P("mp", None),
            P(),
            P(),
            P(),
            P(None, None, "mp"),
            P("mp", None),
            P(),
            P(None, "mp"),
            P("mp", None),
            P("batch", None, "mp", None),
        ),
        out_specs=(
            P("batch", "section", "mp", None),
            P(),
            P(None, ("section", "batch"), "mp"),
            P("mp", ("section", "batch")),
            P(),
            P(("section", "batch"), "mp"),
            P("mp", ("section", "batch")),
            P(),
            P(),
            P(),
            P(None, ("section", "batch"), "mp"),
            P("mp", ("section", "batch")),
            P(),
            P(("section", "batch"), "mp"),
            P("mp", ("section", "batch")),
        ),
        check_vma=False,
    )
```
